32 devices in a mesh: shard: 2 (over y), replica: 16 (over z, x, core).
Axes of the slice: x: 2, y: 2, z: 4, core: 2. Of those that a mesh axis runs over, the one named last changes fastest.
Arguments:
- tokens: bfloat16 [32768, 1024], P(('shard', 'replica')), may hold values from -6 to 6
- cotangent: bfloat16 [32768, 1024], P(('shard', 'replica')), may hold values from -6 to 6
- segment_ids: int32 [32, 1024], P(('shard', 'replica')), may hold values from 0 to 3, never falling along the last dimension, each value on 1 to 800 neighbouring positions
- owners: int32 [96], replicated, may hold values from 0 to 15, as said below
- master: float32 [192, 1024, 128], P('replica', 'shard'), may hold values from -4 to 4
- moment_one: float32 [192, 1024, 128], P('replica', 'shard'), may hold values from -6553.6 to 6553.6
- moment_two: float32 [192, 1024, 128], P('replica', 'shard'), may hold values from 2.62144 to 42.5984
- vectors: float32 [12, 1024], replicated, may hold values from -2 to 2
- vector_one: float32 [12, 1024], replicated, may hold values from -13107.2 to 13107.2
- vector_two: float32 [12, 1024], replicated, may hold values from 8.192 to 131.072
Outputs:
- output: bfloat16 [32768, 1024], P(('shard', 'replica'))
- input_grad: bfloat16 [32768, 1024], P(('shard', 'replica'))
- new_master: float32 [192, 1024, 128], P('replica', 'shard')
- master_copy: bfloat16 [192, 1024, 128], P('replica', 'shard')
- new_one: float32 [192, 1024, 128], P('replica', 'shard')
- new_two: float32 [192, 1024, 128], P('replica', 'shard')
- new_vectors: float32 [12, 1024], replicated
- new_vector_one: float32 [12, 1024], replicated
- new_vector_two: float32 [12, 1024], replicated
The draws below stay inside these ranges and needn't reach their ends.
Inputs may be any that keep to these rules, and one draw needn't show every extreme that they name: owners[j] is the replica that keeps stripe j. One replica keeps exactly 12 stripes; every other keeps at most 12, and the counts of the others differ by at most one. A replica keeps its stripes in its slots in increasing stripe order; its later slots are unused. `segment_ids`: within each sequence segment numbers never fall and each document has 1 to 800 tokens, one exactly 800.
All inputs are finite; a program needn't handle non-finite values.
Results may differ from the reference program's by a relative error of at most 0.018.
Values may be sent and summed in bfloat16 or wider, within the bound.
No kernel may reach another device: no remote copies, remote signals or barrier semaphores. Data moves between devices by JAX's collectives and lax.ppermute only.
A program may use at most 320 MiB of HBM per device.

```python
import math
import jax
import jax.numpy as jnp
import numpy as np
from jax import lax

D = 1024
HEADS = 16
HEAD_DIM = 64
FF = 4096
L = 1024
DOC_MOST = 800
DOCS = 4
SW = 128
STEP = 10
SEQS = 32
TOKENS = 32768
NBLK = 96
MOST = 12
NVEC = 12
N_REPLICA = 16


def stripe_owners(key):
    key = jax.random.fold_in(key, 11)
    first_key, second_key = jax.random.split(key)
    replicas = jax.random.permutation(first_key, N_REPLICA).astype(jnp.int32)
    order = jax.random.permutation(second_key, NBLK).astype(jnp.int32)
    ranks = jnp.arange(NBLK, dtype=jnp.int32)
    others = replicas[1 + (ranks - MOST) % (N_REPLICA - 1)]
    chosen = jnp.where(ranks < MOST, replicas[0], others)
    return jnp.zeros((NBLK,), jnp.int32).at[order].set(chosen)


def draw_owners(key, part):
    return stripe_owners(key)


def draw_master(key, part):
    owners = stripe_owners(key)
    key = jax.random.fold_in(key, 5)
    stripe_ids = jnp.arange(NBLK, dtype=jnp.int32)
    earlier = (owners[None, :] == owners[:, None]) & (stripe_ids[None, :] < stripe_ids[:, None])
    slot_place = owners * MOST + jnp.sum(earlier.astype(jnp.int32), axis=1)
    first_column = stripe_ids * SW
    ratio = (D / FF) ** 0.5
    stripe_scale = jnp.where(first_column < 3 * D, 1.0, jnp.where(first_column < 4 * D, 4.0, jnp.where(first_column < 4 * D + FF, 1.0, 1.5 * ratio))) * D ** (-0.5)
    slot_scale = jnp.full((N_REPLICA * MOST,), D ** (-0.5), jnp.float32).at[slot_place].set(stripe_scale.astype(jnp.float32))
    values = jnp.clip(jax.random.normal(key, (N_REPLICA * MOST, D, SW), jnp.float32), -4.0, 4.0)
    return values * slot_scale[:, None, None]


def draw_moment_one(key, part):
    key = jax.random.fold_in(key, 21)
    values = jnp.clip(jax.random.normal(key, (N_REPLICA * MOST, D, SW), jnp.float32), -4.0, 4.0)
    return values * (0.045 * TOKENS ** 0.5)


def draw_vectors(key, part):
    key = jax.random.fold_in(key, 31)
    first_key, second_key = jax.random.split(key)
    shifts = jnp.clip(jax.random.normal(first_key, (NVEC, D), jnp.float32), -4.0, 4.0) * 0.3
    gains = 1.0 + 0.3 * jax.random.uniform(second_key, (NVEC, D), jnp.float32, -1.0, 1.0)
    row_ids = jnp.arange(NVEC)[:, None]
    return jnp.where((row_ids == 3) | (row_ids == 6), gains, shifts)


def draw_vector_one(key, part):
    key = jax.random.fold_in(key, 41)
    values = jnp.clip(jax.random.normal(key, (NVEC, D), jnp.float32), -4.0, 4.0)
    return values * (0.08 * TOKENS ** 0.5)


def block_levels(stream_key, extent, shards, smallest, top_value):
    factor_of = 1.0
    for position, shards_of in shards:
        steps = jax.random.uniform(jax.random.fold_in(jax.random.fold_in(stream_key, 6), position), (shards_of,), jnp.float32, smallest / len(shards), top_value / len(shards))
        factor_of = factor_of * jnp.repeat(jnp.exp(steps), extent[position] // shards_of).reshape((-1,) + (1,) * (len(extent) - 1 - position))
    return factor_of


def profile(count, total, reach, lean):
    loads = [(1 << 20) // math.isqrt(standing ** lean) + 1 for standing in range(2, count + 1)]
    surplus, given = total - reach - (count - 1), [1] * (count - 1)
    while surplus > 0:
        free = [i for i in range(count - 1) if given[i] < reach]
        pool, left = sum([loads[i] for i in free]), surplus
        for i in free:
            addition = min(reach - given[i], max(1, left * loads[i] // pool), surplus)
            given[i] = given[i] + addition
            surplus = surplus - addition
    return np.array([reach] + given)


def ragged(stream_key, amount, total, bound, lean):
    if amount == 2:
        one = jax.random.randint(stream_key, (), max(1, total - bound), min(bound, total - 1) + 1)
        return jnp.stack([one, total - one])
    tallies = jnp.asarray(profile(amount, total, bound, lean), jnp.int32)
    pairs = (amount - 1) // 2
    donor, receiver = tallies[1:1 + 2 * pairs:2], tallies[2:2 + 2 * pairs:2]
    room = jnp.minimum(donor - 1, bound - receiver)
    moved = jax.random.randint(jax.random.fold_in(stream_key, 1), (pairs,), 0, 1 << 20) % (room + 1)
    tallies = tallies.at[1:1 + 2 * pairs:2].set(donor - moved).at[2:2 + 2 * pairs:2].set(receiver + moved)
    return tallies[jax.random.permutation(jax.random.fold_in(stream_key, 2), amount)]


def normal_values(rng, shape, scale, bound, pieces=(), held_as=jnp.bfloat16):
    loudness = block_levels(rng, shape, pieces, -0.22, 0.18) if pieces else 1.0
    values = jax.random.normal(rng, shape, jnp.float32) * scale * loudness
    return jnp.minimum(jnp.maximum(values, -bound), bound).astype(held_as)


def setup_inputs(seed: int = 0) -> dict:
    key_list = jax.random.split(jax.random.key(seed), 11)
    return {
        "tokens": normal_values(key_list[0], (TOKENS, D), 1.0, 6.0, ((0, 32),)),
        "cotangent": normal_values(key_list[1], (TOKENS, D), 1.0, 6.0, ((0, 32),)),
        "segment_ids": jax.vmap(lambda own: jnp.searchsorted(jnp.cumsum(ragged(own, DOCS, L, DOC_MOST, 2)), jnp.arange(L), side="right"))(jax.random.split(key_list[2], SEQS)).reshape((SEQS, L)).astype(jnp.int32),
        "owners": draw_owners(jax.random.fold_in(key_list[10], 71), 0),
        "master": draw_master(jax.random.fold_in(key_list[10], 71), 0),
        "moment_one": draw_moment_one(jax.random.fold_in(key_list[10], 71), 0),
        "moment_two": jnp.clip(jnp.exp(math.log(42.5984) - 2.7880929 * jax.random.uniform(key_list[6], (N_REPLICA * MOST, D, SW), jnp.float32) ** block_levels(key_list[6], (N_REPLICA * MOST, D, SW), ((0, 16), (1, 2)), -0.2, 0.2)), 2.62144, 42.5984),
        "vectors": draw_vectors(jax.random.fold_in(key_list[10], 71), 0),
        "vector_one": draw_vector_one(jax.random.fold_in(key_list[10], 71), 0),
        "vector_two": jnp.clip(jnp.exp(jax.random.uniform(key_list[9], (NVEC, D), jnp.float32, math.log(8.192), math.log(131.072))), 8.192, 131.072),
    }


@jax.custom_vjp
def low(v):
    return lax.optimization_barrier(v.astype(jnp.bfloat16)).astype(jnp.float32)

@jax.custom_vjp
def low_back(v):
    return v

def low_keep(v):
    return (low(v), None)

def low_pass(kept, grad):
    return (grad,)

def back_keep(v):
    return (v, None)

def back_low(kept, grad):
    return (low(grad),)
low.defvjp(low_keep, low_pass)
low_back.defvjp(back_keep, back_low)
beta_one = 0.9
beta_two = 0.999
epsilon = 1e-08
rate_matrix = 0.05
rate_vector = 0.3
decay_rate = 0.01

def precise_dot(left, right):
    return jnp.dot(left, right, precision=lax.Precision.HIGHEST)

def layer_norm(hidden, gain, shift):
    centered = hidden - lax.optimization_barrier(jnp.mean(hidden, axis=-1, keepdims=True))
    spread = lax.optimization_barrier(jnp.mean(centered * centered, axis=-1, keepdims=True))
    return centered * lax.rsqrt(spread + 1e-05) * gain + shift

def attend(item):
    query_seq, key_seq, value_seq, seg_seq = item
    scale = HEAD_DIM ** (-0.5)
    raw = jnp.einsum('qhd,khd->hqk', query_seq, key_seq, precision=lax.Precision.HIGHEST) * scale
    raw = low_back(raw)
    same = seg_seq[:, None] == seg_seq[None, :]
    masked = jnp.where(same[None], raw, -1e+30)
    top = lax.optimization_barrier(jnp.max(masked, axis=-1, keepdims=True))
    expd = jnp.exp(masked - top)
    probs = expd / lax.optimization_barrier(jnp.sum(expd, axis=-1, keepdims=True))
    return jnp.einsum('hqk,khd->qhd', low(probs), value_seq, precision=lax.Precision.HIGHEST)

def layer_forward(inputs, weights, vectors, segments):
    w_query = weights[:, :D]
    w_key = weights[:, D:2 * D]
    w_value = weights[:, 2 * D:3 * D]
    w_out = weights[:, 3 * D:4 * D]
    w_up = weights[:, 4 * D:4 * D + FF]
    w_down = weights[:, 4 * D + FF:]
    query = low(low_back(precise_dot(inputs, w_query) + vectors[0]))
    keys = low(low_back(precise_dot(inputs, w_key)))
    values = low(low_back(precise_dot(inputs, w_value) + vectors[1]))
    shape_four = (segments.shape[0], L, HEADS, HEAD_DIM)
    context = lax.map(jax.checkpoint(attend), (query.reshape(shape_four), keys.reshape(shape_four), values.reshape(shape_four), segments))
    context = low(low_back(context.reshape(inputs.shape[0], D)))
    attn = low_back(precise_dot(context, w_out) + vectors[2])
    normed = layer_norm(inputs + attn, vectors[3], vectors[4])
    upward = low_back(precise_dot(low(normed), w_up) + vectors[8:].reshape(FF))
    active = low(jax.nn.gelu(upward, approximate=False))
    branch = low_back(precise_dot(active, w_down.T) + vectors[5])
    return layer_norm(normed + branch, vectors[6], vectors[7])

def adamw(param, first, second, grad, rate, decay):
    first = beta_one * first + (1.0 - beta_one) * grad
    second = beta_two * second + (1.0 - beta_two) * grad * grad
    corrected = first / (1.0 - beta_one ** STEP) / (jnp.sqrt(second / (1.0 - beta_two ** STEP)) + epsilon)
    return (param - rate * (corrected + decay * param), first, second)

def reference(tokens, cotangent, segment_ids, owners, master, moment_one, moment_two, vectors, vector_one, vector_two):
    stripe_ids = jnp.arange(NBLK, dtype=jnp.int32)
    earlier = (owners[None, :] == owners[:, None]) & (stripe_ids[None, :] < stripe_ids[:, None])
    slot_of = lax.optimization_barrier(jnp.sum(earlier.astype(jnp.int32), axis=1))
    slot_place = (owners * MOST + slot_of).astype(jnp.int32)
    halves = low(master)
    weights = jnp.take(halves, slot_place, axis=0).transpose(1, 0, 2).reshape(D, NBLK * SW)
    per_scan = 4 if SEQS % 4 == 0 else 1
    scan_steps = SEQS // per_scan
    token_groups = tokens.reshape(scan_steps, per_scan * L, D)
    back_groups = cotangent.reshape(scan_steps, per_scan * L, D)
    seg_groups = segment_ids.reshape(scan_steps, per_scan, L)

    def scan_body(carry, item):
        inputs, backs, segments = item

        def forward(input_values, weight_values, vector_values):
            return layer_forward(input_values, weight_values, vector_values, segments)
        result, pullback = jax.vjp(forward, inputs.astype(jnp.float32), weights, vectors)
        grad_input, grad_weights, grad_vectors = pullback(backs.astype(jnp.float32))
        return ((carry[0] + grad_weights, carry[1] + grad_vectors), (result.astype(jnp.bfloat16), grad_input.astype(jnp.bfloat16)))
    start = (jnp.zeros((D, NBLK * SW), jnp.float32), jnp.zeros((NVEC, D), jnp.float32))
    (weight_grad, vector_grad), (outputs, input_grads) = lax.scan(scan_body, start, (token_groups, back_groups, seg_groups))
    stripes = weight_grad.reshape(D, NBLK, SW).transpose(1, 0, 2)
    slot_grad = jnp.zeros((N_REPLICA * MOST, D, SW), weight_grad.dtype).at[slot_place].set(stripes)
    used = jnp.zeros((N_REPLICA * MOST,), jnp.int32).at[slot_place].set(1) > 0
    keep = used[:, None, None]
    new_master, new_one, new_two = adamw(master, moment_one, moment_two, slot_grad, rate_matrix, decay_rate)
    new_master = jnp.where(keep, new_master, 0.0)
    new_one = jnp.where(keep, new_one, 0.0)
    new_two = jnp.where(keep, new_two, 0.0)
    master_copy = new_master.astype(jnp.bfloat16)
    new_vectors, new_vector_one, new_vector_two = adamw(vectors, vector_one, vector_two, vector_grad, rate_vector, 0.0)
    return (outputs.reshape(TOKENS, D), input_grads.reshape(TOKENS, D), new_master, master_copy, new_one, new_two, new_vectors, new_vector_one, new_vector_two)
```

```python
import functools
import math

import jax
import jax.numpy as jnp
from jax import lax
from jax.experimental import pallas as pl
from jax.experimental.pallas import tpu as pltpu
from jax.sharding import PartitionSpec as P

D = 1024
HEADS = 16
HEAD_DIM = 64
FF = 4096
STEP = 10
PAIR = 2 * HEAD_DIM
BOTH = ("shard", "replica")
VMEM_BYTES = 56 * 1024 * 1024
TILE = 1024
LANES = 128
BLOCKS = D // LANES

beta_one = 0.9
beta_two = 0.999
epsilon = 1e-08
rate_matrix = 0.05
rate_vector = 0.3
decay_rate = 0.01

NT = (((1,), (1,)), ((), ()))
TN = (((0,), (0,)), ((), ()))
EXPONENT = HEAD_DIM ** (-0.5) * math.log2(math.e)


def layer_norm(hidden, gain, shift):
    centered = hidden - jnp.mean(hidden, axis=-1, keepdims=True)
    spread = jnp.mean(centered * centered, axis=-1, keepdims=True)
    return centered * lax.rsqrt(spread + 1e-05) * gain + shift


def adamw(param, first, second, grad, rate, decay):
    first = beta_one * first + (1.0 - beta_one) * grad
    second = beta_two * second + (1.0 - beta_two) * grad * grad
    corrected = (
        first / (1.0 - beta_one**STEP) / (jnp.sqrt(second / (1.0 - beta_two**STEP)) + epsilon)
    )
    return (param - rate * (corrected + decay * param), first, second)


def head_masks():
    lane = lax.broadcasted_iota(jnp.int32, (1, PAIR), 1)
    first = (lane < HEAD_DIM).astype(jnp.float32)
    return (first.astype(jnp.bfloat16), (1.0 - first).astype(jnp.bfloat16))


def make_bias(seg_col_ref, seg_row_ref, bias_ref):
    @pl.when(pl.program_id(0) == 0)
    def _():
        same = seg_col_ref[...] == seg_row_ref[...]
        bias_ref[...] = jnp.where(same, 0.0, -1e30)


def attend_kernel(query_ref, key_ref, value_ref, seg_col_ref, seg_row_ref, context_ref, log_ref, bias_ref):
    make_bias(seg_col_ref, seg_row_ref, bias_ref)
    masks = head_masks()
    keys = key_ref[...]
    values = value_ref[...]
    length = keys.shape[0]
    block = 512
    lane = lax.broadcasted_iota(jnp.int32, (block, PAIR), 1)
    for first_row in range(0, length, block):
        rows = pl.ds(first_row, block)
        query = query_ref[rows, :]
        total = jnp.zeros((block, PAIR), jnp.float32)
        logs = jnp.zeros((block, PAIR), jnp.float32)
        for head, mask in enumerate(masks):
            scores = lax.dot_general(query * mask, keys, NT, preferred_element_type=jnp.float32)
            scores = scores + bias_ref[rows, :]
            top = jnp.max(scores, axis=1, keepdims=True)
            expd = jnp.exp2((scores - top) * EXPONENT)
            norm = jnp.sum(expd, axis=1, keepdims=True)
            part = jnp.dot(expd.astype(jnp.bfloat16), values * mask, preferred_element_type=jnp.float32)
            total = total + part * (1.0 / norm)
            logs = jnp.where(lane == head, top * EXPONENT + jnp.log2(norm), logs)
        context_ref[rows, :] = total.astype(jnp.bfloat16)
        log_ref[0, :, rows] = jnp.transpose(logs)[:8, :]


def kernel_call(kernel, name, grid, in_specs, operands, out_specs, out_shape, scratch, flops, places=None, after=(), aliases=None):
    count, prefetch = len(after), 0 if places is None else 1

    def body(*refs):
        kernel(*refs[:prefetch], *refs[prefetch + count :])

    moved = sum(math.prod(array.shape) * array.dtype.itemsize for array in operands)
    made = jax.tree.leaves(out_shape)
    moved += sum(math.prod(array.shape) * array.dtype.itemsize for array in made)
    return pl.pallas_call(
        body,
        grid_spec=pltpu.PrefetchScalarGridSpec(
            num_scalar_prefetch=prefetch,
            grid=grid,
            in_specs=[pl.BlockSpec(memory_space=pl.ANY)] * count + list(in_specs),
            out_specs=out_specs,
            scratch_shapes=scratch,
        ),
        out_shape=out_shape,
        input_output_aliases={prefetch + count + k: v for k, v in (aliases or {}).items()},
        compiler_params=pltpu.CompilerParams(vmem_limit_bytes=VMEM_BYTES),
        cost_estimate=pl.CostEstimate(flops=flops // 16, bytes_accessed=moved // 16, transcendentals=0),
        name=name,
    )(*([] if places is None else [places]), *after, *operands)


def attend(projected, seg_col, seg_row, first_pair, pair_count, earlier, after=()):
    length = projected.shape[0]
    pairs = D // PAIR

    def spec(offset):
        return pl.BlockSpec((length, PAIR), lambda i: (0, offset + first_pair + i))

    in_specs = [
        spec(0),
        spec(pairs),
        spec(2 * pairs),
        pl.BlockSpec((length, 1), lambda i: (0, 0)),
        pl.BlockSpec((1, length), lambda i: (0, 0)),
    ]
    operands = [projected, projected, projected, seg_col, seg_row]
    kernel, aliases = attend_kernel, None
    if earlier is not None:
        in_specs += [pl.BlockSpec(memory_space=pl.ANY)] * 2
        operands += list(earlier)
        aliases = {5: 0, 6: 1}
        kernel = lambda *refs: attend_kernel(*refs[:5], *refs[7:])
    return kernel_call(
        kernel,
        "attend",
        (pair_count,),
        in_specs,
        operands,
        [spec(0), pl.BlockSpec((1, 8, length), lambda i: (first_pair + i, 0, 0))],
        [
            jax.ShapeDtypeStruct((length, D), jnp.bfloat16),
            jax.ShapeDtypeStruct((pairs, 8, length), jnp.float32),
        ],
        [pltpu.VMEM((length, length), jnp.float32)],
        16 * 2 * pair_count * length * length * HEAD_DIM,
        after=after,
        aliases=aliases,
    )


def attend_back_kernel(
    query_ref, key_ref, value_ref, context_ref, grad_ref, log_ref, seg_col_ref, seg_row_ref,
    grad_ref_all, sum_ref, bias_ref,
):
    make_bias(seg_col_ref, seg_row_ref, bias_ref)
    masks = head_masks()
    query = query_ref[...]
    grad = grad_ref[...]
    length = query.shape[0]
    block = 1024
    row_id = lax.broadcasted_iota(jnp.int32, (8, PAIR), 0)
    lane_id = lax.broadcasted_iota(jnp.int32, (8, PAIR), 1)
    chooser = (lane_id // HEAD_DIM == row_id).astype(jnp.float32)
    product = grad.astype(jnp.float32) * context_ref[...].astype(jnp.float32)
    inner = lax.dot_general(
        chooser, product, NT, precision=lax.Precision.HIGHEST, preferred_element_type=jnp.float32
    )
    grad_query = jnp.zeros((PAIR, length), jnp.float32)
    value_sum = jnp.zeros((1, PAIR), jnp.float32)
    for first_row in range(0, length, block):
        rows = pl.ds(first_row, block)
        keys = key_ref[rows, :]
        values = value_ref[rows, :]
        grad_key = jnp.zeros((block, PAIR), jnp.float32)
        grad_value = jnp.zeros((block, PAIR), jnp.float32)
        for head, mask in enumerate(masks):
            key_head = keys * mask
            scores = lax.dot_general(key_head, query, NT, preferred_element_type=jnp.float32)
            scores = scores + bias_ref[rows, :]
            probs = jnp.exp2(scores * EXPONENT - log_ref[0, head : head + 1, :])
            grad_probs = lax.dot_general(values * mask, grad, NT, preferred_element_type=jnp.float32)
            grad_scores = (probs * (grad_probs - inner[head : head + 1, :])).astype(jnp.bfloat16)
            grad_value = grad_value + jnp.dot(
                probs.astype(jnp.bfloat16), grad * mask, preferred_element_type=jnp.float32
            )
            grad_key = grad_key + jnp.dot(
                grad_scores, query * mask, preferred_element_type=jnp.float32
            )
            grad_query = grad_query + lax.dot_general(
                key_head, grad_scores, TN, preferred_element_type=jnp.float32
            )
        grad_ref_all[1, rows, :] = (grad_key * HEAD_DIM ** (-0.5)).astype(jnp.bfloat16)
        grad_value = grad_value.astype(jnp.bfloat16)
        grad_ref_all[2, rows, :] = grad_value
        value_sum = value_sum + jnp.sum(grad_value.astype(jnp.float32), axis=0, keepdims=True)
    grad_query = jnp.transpose(grad_query * HEAD_DIM ** (-0.5)).astype(jnp.bfloat16)
    grad_ref_all[0] = grad_query
    query_sum = jnp.sum(grad_query.astype(jnp.float32), axis=0, keepdims=True)
    sum_ref[0] = jnp.where(row_id == 0, query_sum, value_sum)


def attend_back(
    projected, context, grad_context, logs, seg_col, seg_row, first_pair, pair_count, half_first, half_count, earlier, after=()
):
    length = projected.shape[0]
    pairs = D // PAIR
    shift = first_pair - half_first

    def spec(offset):
        return pl.BlockSpec((length, PAIR), lambda i: (0, offset + first_pair + i))

    in_specs = [
        spec(0),
        spec(pairs),
        spec(2 * pairs),
        spec(0),
        spec(0),
        pl.BlockSpec((1, 8, length), lambda i: (first_pair + i, 0, 0)),
        pl.BlockSpec((length, 1), lambda i: (0, 0)),
        pl.BlockSpec((1, length), lambda i: (0, 0)),
    ]
    operands = [projected, projected, projected, context, grad_context, logs, seg_col, seg_row]
    kernel, aliases = attend_back_kernel, None
    if earlier is not None:
        in_specs += [pl.BlockSpec(memory_space=pl.ANY)] * 2
        operands += list(earlier)
        aliases = {8: 0, 9: 1}
        kernel = lambda *refs: attend_back_kernel(*refs[:8], *refs[10:])
    return kernel_call(
        kernel,
        "attend_back",
        (pair_count,),
        in_specs,
        operands,
        [
            pl.BlockSpec((3, length, PAIR), lambda i: (0, 0, shift + i)),
            pl.BlockSpec((1, 8, PAIR), lambda i: (shift + i, 0, 0)),
        ],
        [
            jax.ShapeDtypeStruct((3, length, half_count * PAIR), jnp.bfloat16),
            jax.ShapeDtypeStruct((half_count, 8, PAIR), jnp.float32),
        ],
        [pltpu.VMEM((length, length), jnp.float32)],
        40 * 2 * pair_count * length * length * HEAD_DIM,
        after=after,
        aliases=aliases,
    )


def joined(piece_refs):
    if len(piece_refs) == 1:
        return piece_refs[0][...]
    return jnp.concatenate([ref[...] for ref in piece_refs], axis=0)


def block_at(place_ref, index):
    return pl.ds(pl.multiple_of(place_ref[index] * LANES, LANES), LANES)


def to_pieces(place_ref, from_ref, to_ref):
    for index in range(BLOCKS):
        to_ref[:, index * LANES : (index + 1) * LANES] = from_ref[:, block_at(place_ref, index)]


def from_pieces(place_ref, from_ref, to_ref):
    for index in range(BLOCKS):
        part = from_ref[:, index * LANES : (index + 1) * LANES]
        to_ref[:, block_at(place_ref, index)] = part.astype(to_ref.dtype)


def tile_specs(pieces, tile_of):
    return [pl.BlockSpec((piece.shape[0], TILE), lambda j, *_: (0, tile_of(j))) for piece in pieces]


def whole(*shape):
    return pl.BlockSpec(shape, lambda j, *_: (0,) * len(shape))


ANYWHERE = pl.BlockSpec(memory_space=pl.ANY)


def whole_once(*shape):
    return pl.BlockSpec(shape, lambda j, *_: (0,) * len(shape), pipeline_mode=pl.Buffered(1))


def project_kernel(place_ref, input_ref, bias_ref, *refs):
    pieces, (out_ref, turned_ref) = refs[:-2], refs[-2:]

    @pl.when(pl.program_id(0) == 0)
    def _():
        to_pieces(place_ref, input_ref, turned_ref)

    weights, bias = joined(pieces), bias_ref[...]
    block = 512
    for first_row in range(0, turned_ref.shape[0], block):
        rows = pl.ds(first_row, block)
        made = jnp.dot(turned_ref[rows, :], weights, preferred_element_type=jnp.float32)
        out_ref[rows, :] = (made + bias).astype(jnp.bfloat16)


def project(inputs, bias, weight, places, after=()):
    rows = inputs.shape[0]
    columns = weight[0].shape[1]
    return kernel_call(
        project_kernel,
        "project",
        (columns // TILE,),
        [whole_once(rows, D), pl.BlockSpec((1, TILE), lambda j, *_: (0, j))] + tile_specs(weight, lambda j: j),
        [inputs, bias, *weight],
        pl.BlockSpec((rows, TILE), lambda j, *_: (0, j)),
        jax.ShapeDtypeStruct((rows, columns), jnp.bfloat16),
        [pltpu.VMEM((rows, D), jnp.bfloat16)],
        2 * rows * D * columns,
        places=places,
        after=after,
    )


def row_loop(rows_all, block, body, start):
    def step(index, carry):
        return body(pl.ds(pl.multiple_of(index * block, block), block), carry)

    return lax.fori_loop(0, rows_all // block, step, start)


def gelu_tile(turned_ref, weights, bias, active_ref, slope_ref):
    block = 512
    for first_row in range(0, turned_ref.shape[0], block):
        rows = pl.ds(first_row, block)
        upward = jnp.dot(turned_ref[rows, :], weights, preferred_element_type=jnp.float32) + bias
        cumulative = 0.5 + 0.5 * lax.erf(upward * (2.0**-0.5))
        density = jnp.exp2(upward * upward * (-0.5 * math.log2(math.e))) * (2.0 * math.pi) ** -0.5
        active_ref[rows, :] = (upward * cumulative).astype(jnp.bfloat16)
        slope_ref[rows, :] = (cumulative + upward * density).astype(jnp.bfloat16)


def out_up_kernel(place_ref, vector_ref, bias_ref, context_ref, token_ref, *refs):
    pieces = refs[:-10]
    unit_out, spread_ref, low_out, active_ref, slope_ref, turned_ref, attn_ref, unit_ref, low_ref, sems = refs[-10:]
    step = pl.program_id(0)
    rows_all = context_ref.shape[0]

    def leaving():
        return [
            pltpu.make_async_copy(unit_ref, unit_out, sems.at[0]),
            pltpu.make_async_copy(low_ref, low_out, sems.at[1]),
        ]

    @pl.when(step == 0)
    def _():
        to_pieces(place_ref, context_ref, turned_ref)
        attn_ref[...] = jnp.dot(turned_ref[...], joined(pieces), preferred_element_type=jnp.float32)

        def normalise(rows, carry):
            hidden = token_ref[rows, :].astype(jnp.float32) + (attn_ref[rows, :] + vector_ref[2:3, :])
            centered = hidden - jnp.mean(hidden, axis=1, keepdims=True)
            spread = lax.rsqrt(jnp.mean(centered * centered, axis=1, keepdims=True) + 1e-05)
            unit = centered * spread
            unit_ref[rows, :] = unit
            spread_ref[rows, :] = jnp.broadcast_to(spread, (unit.shape[0], LANES))
            low_ref[rows, :] = (unit * vector_ref[3:4, :] + vector_ref[4:5, :]).astype(jnp.bfloat16)
            return carry

        row_loop(rows_all, 128, normalise, 0)
        for copy in leaving():
            copy.start()
        to_pieces(place_ref, low_ref, turned_ref)

    @pl.when(step > 0)
    def _():
        gelu_tile(turned_ref, joined(pieces), bias_ref[...], active_ref, slope_ref)

    @pl.when(step == pl.num_programs(0) - 1)
    def _():
        for copy in leaving():
            copy.wait()


def out_up(context, tokens, vectors, up_bias, weight, places, up_tiles, after=()):
    rows = context.shape[0]
    late = lambda j, *_: (0, jnp.maximum(j - 1, 0))
    return kernel_call(
        out_up_kernel,
        "out_up",
        (1 + up_tiles,),
        [whole_once(*vectors.shape), pl.BlockSpec((1, TILE), late), whole_once(rows, D), whole_once(rows, D)]
        + tile_specs(weight, lambda j: j),
        [vectors, up_bias, context, tokens, *weight],
        [
            ANYWHERE,
            whole(rows, LANES),
            ANYWHERE,
            pl.BlockSpec((rows, TILE), late),
            pl.BlockSpec((rows, TILE), late),
        ],
        [
            jax.ShapeDtypeStruct((rows, D), jnp.float32),
            jax.ShapeDtypeStruct((rows, LANES), jnp.float32),
            jax.ShapeDtypeStruct((rows, D), jnp.bfloat16),
            jax.ShapeDtypeStruct((rows, FF), jnp.bfloat16),
            jax.ShapeDtypeStruct((rows, FF), jnp.bfloat16),
        ],
        [
            pltpu.VMEM((rows, D), jnp.bfloat16),
            pltpu.VMEM((rows, D), jnp.float32),
            pltpu.VMEM((rows, D), jnp.float32),
            pltpu.VMEM((rows, D), jnp.bfloat16),
            pltpu.SemaphoreType.DMA((2,)),
        ],
        2 * rows * D * (1 + up_tiles) * TILE,
        places=places,
        after=after,
    )


def up_rest_kernel(place_ref, bias_ref, low_ref, *refs):
    pieces, (active_ref, slope_ref, turned_ref) = refs[:-5], refs[-3:]

    @pl.when(pl.program_id(0) == 0)
    def _():
        to_pieces(place_ref, low_ref, turned_ref)

    gelu_tile(turned_ref, joined(pieces), bias_ref[...], active_ref, slope_ref)


def up_rest(normed_low, up_bias, weight, places, first_tile, filled, after=()):
    rows = normed_low.shape[0]
    at = lambda j, *_: (0, first_tile + j)
    tiles = FF // TILE - first_tile
    count = len(weight)
    return kernel_call(
        up_rest_kernel,
        "up_rest",
        (tiles,),
        [pl.BlockSpec((1, TILE), at), whole_once(rows, D)]
        + tile_specs(weight, lambda j: 1 + first_tile + j)
        + [pl.BlockSpec(memory_space=pl.ANY)] * 2,
        [up_bias, normed_low, *weight, *filled],
        [pl.BlockSpec((rows, TILE), at)] * 2,
        [jax.ShapeDtypeStruct((rows, FF), jnp.bfloat16)] * 2,
        [pltpu.VMEM((rows, D), jnp.bfloat16)],
        2 * rows * D * tiles * TILE,
        places=places,
        after=after,
        aliases={2 + count: 0, 3 + count: 1},
    )


def column_sum(values):
    return jnp.sum(values, axis=0, keepdims=True)


def down_kernel(place_ref, vector_ref, unit_in, cotangent_in, active_ref, slope_ref, *refs):
    pieces, (out_out, second_out, branch_out, grad_up_ref, sum_ref, up_sum_ref) = refs[:-14], refs[-14:-8]
    total_ref, turned_ref, unit_ref, cotangent_ref, out_ref, second_ref, branch_ref, sems = refs[-8:]
    step = pl.program_id(0)
    rows_all = active_ref.shape[0]
    tiles = FF // TILE

    def coming():
        return [
            pltpu.make_async_copy(unit_in, unit_ref, sems.at[0]),
            pltpu.make_async_copy(cotangent_in, cotangent_ref, sems.at[1]),
        ]

    def leaving():
        return [
            pltpu.make_async_copy(out_ref, out_out, sems.at[2]),
            pltpu.make_async_copy(second_ref, second_out, sems.at[3]),
            pltpu.make_async_copy(branch_ref, branch_out, sems.at[4]),
        ]

    @pl.when(step == 0)
    def _():
        for copy in coming():
            copy.start()
        total_ref[...] = lax.dot_general(
            active_ref[...], joined(pieces), NT, preferred_element_type=jnp.float32
        )

    @pl.when((step > 0) & (step < tiles))
    def _():
        total_ref[...] += lax.dot_general(
            active_ref[...], joined(pieces), NT, preferred_element_type=jnp.float32
        )

    @pl.when(step == tiles)
    def _():
        from_pieces(place_ref, total_ref, second_ref)
        for copy in coming():
            copy.wait()

        def normalise(rows, carry):
            normed = unit_ref[rows, :] * vector_ref[3:4, :] + vector_ref[4:5, :]
            hidden = normed + (second_ref[rows, :] + vector_ref[5:6, :])
            centered = hidden - jnp.mean(hidden, axis=1, keepdims=True)
            spread = lax.rsqrt(jnp.mean(centered * centered, axis=1, keepdims=True) + 1e-05)
            unit = centered * spread
            out_ref[rows, :] = (unit * vector_ref[6:7, :] + vector_ref[7:8, :]).astype(jnp.bfloat16)
            grad = cotangent_ref[rows, :].astype(jnp.float32)
            scaled = grad * vector_ref[6:7, :]
            mean_one = jnp.mean(scaled, axis=1, keepdims=True)
            mean_two = jnp.mean(scaled * unit, axis=1, keepdims=True)
            second = spread * (scaled - mean_one - unit * mean_two)
            second_ref[rows, :] = second
            branch = second.astype(jnp.bfloat16)
            branch_ref[rows, :] = branch
            return (
                carry[0] + column_sum(branch.astype(jnp.float32)),
                carry[1] + column_sum(grad * unit),
                carry[2] + column_sum(grad),
            )

        zero = jnp.zeros((1, D), jnp.float32)
        sums = row_loop(rows_all, 128, normalise, (zero, zero, zero))
        for index, value in enumerate(sums):
            sum_ref[index : index + 1, :] = value
        for copy in leaving():
            copy.start()
        to_pieces(place_ref, branch_ref, turned_ref)

    @pl.when(step >= tiles)
    def _():
        grad = jnp.dot(turned_ref[...], joined(pieces), preferred_element_type=jnp.float32)
        grad = (grad * slope_ref[...].astype(jnp.float32)).astype(jnp.bfloat16)
        grad_up_ref[...] = grad
        up_sum_ref[...] = column_sum(grad.astype(jnp.float32))

    @pl.when(step == 2 * tiles - 1)
    def _():
        for copy in leaving():
            copy.wait()


def down_both(unit, cotangent, active, slope, vectors, weight, places, after=()):
    rows = unit.shape[0]
    tiles = FF // TILE
    early = lambda j, *_: (0, jnp.minimum(j, tiles - 1))
    late = lambda j, *_: (0, jnp.maximum(j - tiles, 0))
    return kernel_call(
        down_kernel,
        "down_both",
        (2 * tiles,),
        [
            whole_once(*vectors.shape),
            ANYWHERE,
            ANYWHERE,
            pl.BlockSpec((rows, TILE), early),
            pl.BlockSpec((rows, TILE), late),
        ]
        + tile_specs(weight, lambda j: j % tiles),
        [vectors, unit, cotangent, active, slope, *weight],
        [
            ANYWHERE,
            ANYWHERE,
            ANYWHERE,
            pl.BlockSpec((rows, TILE), late),
            whole(8, D),
            pl.BlockSpec((1, TILE), late),
        ],
        [
            jax.ShapeDtypeStruct((rows, D), jnp.bfloat16),
            jax.ShapeDtypeStruct((rows, D), jnp.float32),
            jax.ShapeDtypeStruct((rows, D), jnp.bfloat16),
            jax.ShapeDtypeStruct((rows, FF), jnp.bfloat16),
            jax.ShapeDtypeStruct((8, D), jnp.float32),
            jax.ShapeDtypeStruct((1, FF), jnp.float32),
        ],
        [
            pltpu.VMEM((rows, D), jnp.float32),
            pltpu.VMEM((rows, D), jnp.bfloat16),
            pltpu.VMEM((rows, D), jnp.float32),
            pltpu.VMEM((rows, D), jnp.bfloat16),
            pltpu.VMEM((rows, D), jnp.bfloat16),
            pltpu.VMEM((rows, D), jnp.float32),
            pltpu.VMEM((rows, D), jnp.bfloat16),
            pltpu.SemaphoreType.DMA((5,)),
        ],
        4 * rows * D * FF,
        places=places,
        after=after,
    )


def up_back_kernel(place_ref, vector_ref, unit_in, spread_ref, second_in, grad_up_ref, *refs):
    pieces, (first_out, attn_out, context_ref, sum_ref) = refs[:-10], refs[-10:-6]
    total_ref, unit_ref, second_ref, first_ref, attn_ref, sems = refs[-6:]
    step = pl.program_id(0)
    rows_all = unit_ref.shape[0]
    tiles = FF // TILE
    out_tiles = D // TILE

    def product(left):
        return lax.dot_general(left, joined(pieces), NT, preferred_element_type=jnp.float32)

    def coming():
        return [
            pltpu.make_async_copy(unit_in, unit_ref, sems.at[0]),
            pltpu.make_async_copy(second_in, second_ref, sems.at[1]),
        ]

    def leaving():
        return [
            pltpu.make_async_copy(first_ref, first_out, sems.at[2]),
            pltpu.make_async_copy(attn_ref, attn_out, sems.at[3]),
        ]

    @pl.when(step == 0)
    def _():
        for copy in coming():
            copy.start()
        total_ref[...] = product(grad_up_ref[...])

    @pl.when((step > 0) & (step < tiles))
    def _():
        total_ref[...] += product(grad_up_ref[...])

    @pl.when(step == tiles)
    def _():
        from_pieces(place_ref, total_ref, first_ref)
        for copy in coming():
            copy.wait()

        def normalise(rows, carry):
            grad = second_ref[rows, :] + first_ref[rows, :]
            unit = unit_ref[rows, :]
            scaled = grad * vector_ref[3:4, :]
            mean_one = jnp.mean(scaled, axis=1, keepdims=True)
            mean_two = jnp.mean(scaled * unit, axis=1, keepdims=True)
            first = spread_ref[rows, :1] * (scaled - mean_one - unit * mean_two)
            first_ref[rows, :] = first
            attn = first.astype(jnp.bfloat16)
            attn_ref[rows, :] = attn
            return (
                carry[0] + column_sum(attn.astype(jnp.float32)),
                carry[1] + column_sum(grad * unit),
                carry[2] + column_sum(grad),
            )

        zero = jnp.zeros((1, D), jnp.float32)
        sums = row_loop(rows_all, 128, normalise, (zero, zero, zero))
        for index, value in enumerate(sums):
            sum_ref[index : index + 1, :] = value
        for copy in leaving():
            copy.start()

    for tile in range(out_tiles):

        @pl.when(step == tiles + tile)
        def _():
            made = product(attn_ref[:, tile * TILE : (tile + 1) * TILE])
            total_ref[...] = made if tile == 0 else total_ref[...] + made

    @pl.when(step == tiles + out_tiles - 1)
    def _():
        from_pieces(place_ref, total_ref, context_ref)
        for copy in leaving():
            copy.wait()


def up_back(unit, spread, second, grad_up, vectors, weight, places, after=()):
    rows = unit.shape[0]
    tiles = FF // TILE
    out_tiles = D // TILE
    return kernel_call(
        up_back_kernel,
        "up_back",
        (tiles + out_tiles,),
        [
            whole_once(*vectors.shape),
            ANYWHERE,
            whole_once(rows, LANES),
            ANYWHERE,
            pl.BlockSpec((rows, TILE), lambda j, *_: (0, jnp.minimum(j, tiles - 1))),
        ]
        + tile_specs(weight, lambda j: (j + out_tiles) % (tiles + out_tiles)),
        [vectors, unit, spread, second, grad_up, *weight],
        [ANYWHERE, ANYWHERE, whole(rows, D), whole(8, D)],
        [
            jax.ShapeDtypeStruct((rows, D), jnp.float32),
            jax.ShapeDtypeStruct((rows, D), jnp.bfloat16),
            jax.ShapeDtypeStruct((rows, D), jnp.bfloat16),
            jax.ShapeDtypeStruct((8, D), jnp.float32),
        ],
        [
            pltpu.VMEM((rows, D), jnp.float32),
            pltpu.VMEM((rows, D), jnp.float32),
            pltpu.VMEM((rows, D), jnp.float32),
            pltpu.VMEM((rows, D), jnp.float32),
            pltpu.VMEM((rows, D), jnp.bfloat16),
            pltpu.SemaphoreType.DMA((4,)),
        ],
        2 * rows * D * (D + FF),
        places=places,
        after=after,
    )


def input_back_kernel(place_ref, first_in, one_ref, two_ref, *refs):
    pieces, (out_ref, total_ref, first_ref, sem) = refs[:-4], refs[-4:]
    step = pl.program_id(0)
    coming = pltpu.make_async_copy(first_in, first_ref, sem)

    def product():
        grad = jnp.concatenate([one_ref[0], two_ref[0]], axis=1)
        return lax.dot_general(grad, joined(pieces), NT, preferred_element_type=jnp.float32)

    @pl.when(step == 0)
    def _():
        coming.start()
        total_ref[...] = product()

    @pl.when(step > 0)
    def _():
        total_ref[...] += product()

    @pl.when(step == 2)
    def _():
        coming.wait()
        for index in range(BLOCKS):
            columns = block_at(place_ref, index)
            part = first_ref[:, columns] + total_ref[:, index * LANES : (index + 1) * LANES]
            out_ref[:, columns] = part.astype(jnp.bfloat16)


def input_back(first, grad_one, grad_two, weight, places, after=()):
    rows = first.shape[0]
    half = pl.BlockSpec((1, rows, D // 2), lambda j, *_: (j, 0, 0))
    return kernel_call(
        input_back_kernel,
        "input_back",
        (3,),
        [ANYWHERE, half, half] + tile_specs(weight, lambda j: j),
        [first, grad_one, grad_two, *weight],
        whole(rows, D),
        jax.ShapeDtypeStruct((rows, D), jnp.bfloat16),
        [pltpu.VMEM((rows, D), jnp.float32), pltpu.VMEM((rows, D), jnp.float32), pltpu.SemaphoreType.DMA],
        2 * rows * D * 3 * D,
        places=places,
        after=after,
    )


def weight_grad_kernel(place_ref, *refs, spans):
    count = len(spans)
    left_refs, right_refs = refs[:count], refs[count : 2 * count]
    out_refs, turned_ref = refs[2 * count : -1], refs[-1]
    step = pl.program_id(0)
    for index, (first, last) in enumerate(spans):

        @pl.when(step == first)
        def _():
            for place in range(BLOCKS):
                turned_ref[pl.ds(place * LANES, LANES), :] = jnp.transpose(
                    left_refs[index][:, block_at(place_ref, place)]
                )

        @pl.when((step >= first) & (step < last))
        def _():
            grad = jnp.dot(turned_ref[...], right_refs[index][0], preferred_element_type=jnp.float32)
            grad = grad.astype(jnp.bfloat16)
            first_row = 0
            for out_ref in out_refs:
                out_ref[...] = grad[first_row : first_row + out_ref.shape[0]]
                first_row += out_ref.shape[0]


def weight_grad(pairs, places, after=()):
    rows = pairs[0][0].shape[0]
    tile_width = min(TILE, *[right.shape[2] for _, right in pairs])
    in_specs, right_specs, operands, rights, spans = [], [], [], [], []
    step = 0
    for left, right in pairs:
        groups, _, width = right.shape
        per_group = width // tile_width
        first, last = step, step + groups * per_group
        step = last
        spans.append((first, last))
        in_specs.append(whole_once(rows, D))
        operands.append(left)

        def right_at(j, place, first=first, last=last, per_group=per_group):
            tile = jnp.clip(j - first, 0, last - first - 1)
            return (tile // per_group, 0, tile % per_group)

        right_specs.append(pl.BlockSpec((1, rows, tile_width), right_at))
        rights.append(right)
    columns = step * tile_width
    heights = [LANES] * 3 + [LANES // 2] * 2 + [4 * LANES]
    return kernel_call(
        functools.partial(weight_grad_kernel, spans=spans),
        "weight_grad",
        (step,),
        in_specs + right_specs,
        operands + rights,
        [pl.BlockSpec((height, tile_width), lambda j, place: (0, j)) for height in heights],
        [jax.ShapeDtypeStruct((height, columns), jnp.bfloat16) for height in heights],
        [pltpu.VMEM((D, rows), jnp.bfloat16)],
        2 * D * rows * columns,
        places=places,
        after=after,
    )


def gate(value, *others):
    return lax.optimization_barrier((value, *others))[0]


def picked(array, places):
    return array.at[places].get(mode="promise_in_bounds")


def wide(value):
    return value.astype(jnp.float32)


class WholeMesh:
    def __init__(self, shard_count, replica_count):
        self.replica_count = replica_count
        self.places = jnp.arange(BLOCKS, dtype=jnp.int32)

    def split_rows(self, slots, slab):
        count, _, width = slots.shape
        return slots.reshape(count, self.replica_count, slab, width).transpose(1, 0, 2, 3)

    def join_rows(self, slabs):
        replicas, count, slab, width = slabs.shape
        return slabs.transpose(1, 0, 2, 3).reshape(count, replicas * slab, width)

    def spread(self, slots, owners, slot_of, slab):
        sent = self.split_rows(slots, slab)
        heard = lax.all_to_all(sent, "replica", split_axis=0, concat_axis=0, tiled=True)
        return picked(heard.reshape(-1, *heard.shape[2:]), owners * slots.shape[0] + slot_of)

    def collect(self, stripes, stripe_at, heavy):
        sent = picked(stripes, stripe_at)
        return self.join_rows(lax.all_to_all(sent, "replica", split_axis=0, concat_axis=0, tiled=True))

    def gather_line(self, mine):
        return lax.all_gather(mine, BOTH, axis=0, tiled=True)

    def gather_near(self, block):
        return [block]

    def gather_far(self, pieces):
        return []

    def gather_core(self, pieces):
        return []

    def scatter_core(self, pairs, after=()):
        parts = [
            lax.dot_general(left, group, TN, preferred_element_type=jnp.float32)
            for left, right in pairs
            for group in right
        ]
        part = jnp.concatenate(parts, axis=1).astype(jnp.bfloat16)
        return [lax.psum_scatter(part, BOTH, scatter_dimension=0, tiled=True)]

    def scatter_near(self, parts):
        return parts

    def scatter_far(self, parts):
        return parts

    def scatter_half(self, parts):
        return parts

    def scatter_slab(self, parts):
        return parts

    def scatter_line(self, parts):
        return parts

    def scatter_end(self, parts):
        return parts[0]

    def total_step(self, part, kind):
        return jnp.sum(lax.all_gather(part, BOTH, axis=0), axis=0) if kind == "core" else part


class BlockMesh:
    def __init__(self, shard_count, replica_count):
        index = lax.axis_index("replica")
        self.y = lax.axis_index("shard")
        self.z, self.x, self.core = index // 4, (index // 2) % 2, index % 2

        def places(core):
            return [
                (self.y ^ dy) * 4 + core * 2 + (self.x ^ dx) for dx, dy in ((0, 0), (1, 0), (0, 1), (1, 1))
            ]

        self.own = jnp.stack(places(self.core)).astype(jnp.int32)
        self.partner = jnp.stack(places(1 - self.core)).astype(jnp.int32)
        self.places = jnp.concatenate([self.own, self.partner])

    def swap(self, array, bits):
        return lax.ppermute(array, "replica", [(r, r ^ bits) for r in range(16)])

    def swap_core(self, array):
        return self.swap(array, 1)

    def swap_x(self, array):
        return self.swap(array, 2)

    def swap_y(self, array):
        return lax.ppermute(array, "shard", [(0, 1), (1, 0)])

    def swap_z(self, array, bits):
        return self.swap(array, 4 * bits)

    def split_rows(self, slots, slab):
        count, _, width = slots.shape
        parts = slots.reshape(count, 2, 2, 4, slab, width).transpose(3, 2, 1, 0, 4, 5)
        return parts.reshape(16, count, slab, width)

    def join_rows(self, slabs):
        _, count, slab, width = slabs.shape
        parts = slabs.reshape(4, 2, 2, count, slab, width).transpose(3, 2, 1, 0, 4, 5)
        return parts.reshape(count, 16 * slab, width)

    def spread(self, slots, owners, slot_of, slab):
        count = owners.shape[0] // 16
        sent = self.split_rows(slots[:count], slab)
        heard = lax.all_to_all(sent, "replica", split_axis=0, concat_axis=0, tiled=True)
        rest = self.split_rows(slots[count:], slab)
        rest = rest.reshape(4, 2, 2, *rest.shape[1:])
        heavy = jnp.max(jnp.where(slot_of >= count, owners, 0))
        odd = self.core == 1
        keep, send = jnp.where(odd, rest[:, :, 1], rest[:, :, 0]), jnp.where(odd, rest[:, :, 0], rest[:, :, 1])
        rest = jnp.where(heavy % 2 == self.core, keep, self.swap_core(send))
        odd = self.x == 1
        keep, send = jnp.where(odd, rest[:, 1], rest[:, 0]), jnp.where(odd, rest[:, 0], rest[:, 1])
        rest = jnp.where((heavy // 2) % 2 == self.x, keep, self.swap_x(send))
        away = (heavy // 4) ^ self.z
        last = lax.dynamic_index_in_dim(rest, self.z, 0, keepdims=False)
        for bits in (1, 2, 3):
            other = lax.dynamic_index_in_dim(rest, self.z ^ bits, 0, keepdims=False)
            last = jnp.where(away == bits, self.swap_z(other, bits), last)
        heard = jnp.concatenate([heard.reshape(-1, *heard.shape[2:]), last], axis=0)
        place = jnp.where(slot_of < count, owners * count + slot_of, 16 * count + slot_of - count)
        return picked(heard, place)

    def collect(self, stripes, stripe_at, heavy):
        count = stripes.shape[0] // 16
        sent = picked(stripes, stripe_at[:, :count])
        extra = lax.dynamic_index_in_dim(stripe_at, heavy, 0, keepdims=False)[count:]
        rest = picked(gate(stripes, sent), extra)
        heard = lax.all_to_all(sent, "replica", split_axis=0, concat_axis=0, tiled=True)
        rest = jnp.stack(self.in_order([rest] + [self.swap_z(rest, bits) for bits in (1, 2, 3)]))
        other = self.swap_x(rest)
        odd = self.x == 1
        rest = jnp.stack([jnp.where(odd, other, rest), jnp.where(odd, rest, other)], axis=1)
        other = self.swap_core(rest)
        odd = self.core == 1
        rest = jnp.stack([jnp.where(odd, other, rest), jnp.where(odd, rest, other)], axis=2)
        rest = rest.reshape(16, *rest.shape[3:])
        return jnp.concatenate([self.join_rows(heard), self.join_rows(rest)], axis=0)

    def in_order(self, heard):
        odd, upper = self.z % 2 == 1, self.z >= 2
        low = [jnp.where(odd, heard[1], heard[0]), jnp.where(odd, heard[0], heard[1])]
        high = [jnp.where(odd, heard[3], heard[2]), jnp.where(odd, heard[2], heard[3])]
        return [jnp.where(upper, b, a) for a, b in zip(low, high)] + [
            jnp.where(upper, a, b) for a, b in zip(low, high)
        ]

    def gather_line(self, mine):
        heard = [mine] + [self.swap_z(mine, bits) for bits in (1, 2, 3)]
        return jnp.concatenate(self.in_order(heard), axis=0)

    def gather_near(self, quarter):
        return [quarter, self.swap_x(quarter), self.swap_y(quarter)]

    def gather_far(self, pieces):
        half = pieces[0].shape[0] // 2
        return [self.swap_y(pieces[1][:half]), self.swap_x(pieces[2][half:])]

    def gather_core(self, pieces):
        return [self.swap_core(piece) for piece in pieces]

    def scatter_core(self, pairs, after=()):
        *parts, partner = weight_grad(pairs, self.places, after=after)
        return [*parts, self.swap_core(partner)]

    def scatter_near(self, parts):
        own, for_x, for_y, far_one, far_two, heard = parts
        rows, half = own.shape[0], far_one.shape[0]
        far_one = (wide(far_one) + wide(heard[3 * rows : 3 * rows + half])).astype(jnp.bfloat16)
        far_two = (wide(far_two) + wide(heard[3 * rows + half :])).astype(jnp.bfloat16)
        return [own, for_x, for_y, heard, self.swap_x(far_one), self.swap_y(far_two)]

    def scatter_far(self, parts):
        own, for_x, for_y, heard, add_y, add_x = parts
        rows, half = own.shape[0], add_y.shape[0]
        heard_x, heard_y = wide(heard[rows : 2 * rows]), wide(heard[2 * rows : 3 * rows])
        for_x, for_y = wide(for_x) + heard_x, wide(for_y) + heard_y
        for_y = jnp.concatenate([for_y[:half] + wide(add_y), for_y[half:]], axis=0)
        for_x = jnp.concatenate([for_x[:half], for_x[half:] + wide(add_x)], axis=0)
        return [
            own,
            heard[:rows],
            self.swap_x(for_x.astype(jnp.bfloat16)),
            self.swap_y(for_y.astype(jnp.bfloat16)),
        ]

    def scatter_half(self, parts):
        quarter = sum(wide(part) for part in parts).astype(jnp.bfloat16)
        half, upper = quarter.shape[0] // 2, self.z // 2
        send = lax.dynamic_slice_in_dim(quarter, (1 - upper) * half, half, axis=0)
        return [lax.dynamic_slice_in_dim(quarter, upper * half, half, axis=0), self.swap_z(send, 2)]

    def scatter_slab(self, parts):
        both = wide(parts[0]) + wide(parts[1])
        slab, odd = both.shape[0] // 2, self.z % 2
        send = lax.dynamic_slice_in_dim(both, (1 - odd) * slab, slab, axis=0).astype(jnp.bfloat16)
        return [lax.dynamic_slice_in_dim(both, odd * slab, slab, axis=0), self.swap_z(send, 1)]

    def scatter_line(self, parts):
        quarter = sum(wide(part) for part in parts).astype(jnp.bfloat16)
        slab = quarter.shape[0] // 4

        def slab_of(bits):
            return lax.dynamic_slice_in_dim(quarter, (self.z ^ bits) * slab, slab, axis=0)

        return [slab_of(0)] + [self.swap_z(slab_of(bits), bits) for bits in (1, 2, 3)]

    def scatter_end(self, parts):
        total = wide(parts[0])
        for part in parts[1:]:
            total = total + wide(part)
        return total.astype(jnp.bfloat16)

    def total_step(self, part, kind):
        swaps = {
            "core": self.swap_core,
            "x": self.swap_x,
            "y": self.swap_y,
            "near z": lambda value: self.swap_z(value, 1),
            "far z": lambda value: self.swap_z(value, 2),
        }
        return part + swaps[kind](part)


def mesh_plan(shard_count, replica_count):
    kind = BlockMesh if (shard_count, replica_count) == (2, 16) else WholeMesh
    return kind(shard_count, replica_count)


def on_device(
    tokens,
    cotangent,
    segment_ids,
    owners,
    master,
    moment_one,
    moment_two,
    vectors,
    vector_one,
    vector_two,
):
    replica_count = lax.axis_size("replica")
    replica_index = lax.axis_index("replica")
    shard_count = lax.axis_size("shard")
    slot_count, shard_rows, stripe = master.shape
    columns = 4 * D + 2 * FF
    stripe_count = columns // stripe
    slab = shard_rows // replica_count
    stripe_ids = jnp.arange(stripe_count, dtype=jnp.int32)
    earlier = (owners[None, :] == owners[:, None]) & (stripe_ids[None, :] < stripe_ids[:, None])
    slot_of = jnp.sum(earlier.astype(jnp.int32), axis=1)
    slot_place = owners * slot_count + slot_of
    places = jnp.arange(replica_count * slot_count, dtype=jnp.int32)
    matches = (slot_place[None, :] == places[:, None]).astype(jnp.int32)
    stripe_at = jnp.sum(matches * stripe_ids[None, :], axis=1).reshape(replica_count, slot_count)
    used = jnp.sum(matches, axis=1) > 0
    heavy = jnp.max(jnp.where(slot_of == slot_count - 1, owners, 0))

    plan = mesh_plan(shard_count, replica_count)
    halves = master.astype(jnp.bfloat16)
    mine = plan.spread(halves, owners, slot_of, slab).transpose(1, 0, 2).reshape(slab, columns)
    up_bias = vectors[8:].reshape(1, FF)
    length = segment_ids.shape[1]
    seg_row = segment_ids.reshape(1, length)
    seg_col = segment_ids.reshape(length, 1)
    places = plan.places
    qkv_bias = jnp.concatenate([vectors[0], jnp.zeros((D,), jnp.float32), vectors[1]])[None]

    near_qkv = plan.gather_near(plan.gather_line(mine[:, : 3 * D]))
    core_qkv = plan.gather_core(near_qkv[:1])
    line_up = plan.gather_line(gate(mine[:, 3 * D : 4 * D + FF], core_qkv))
    far_qkv = plan.gather_far(near_qkv)
    core_qkv = [*core_qkv, *plan.gather_core(near_qkv[1:])]
    w_qkv = [*near_qkv, *far_qkv, *core_qkv, *plan.gather_core(far_qkv)]
    projected = project(tokens, qkv_bias, w_qkv, places)
    near_up = plan.gather_near(gate(line_up, far_qkv))
    line_down = plan.gather_line(gate(mine[:, 4 * D + FF :], projected))
    done = attend(projected, seg_col, seg_row, 0, 2, None)
    far_up = plan.gather_far(gate(near_up, done))
    done = attend(projected, seg_col, seg_row, 2, 2, done, after=near_up[1:])
    done = attend(projected, seg_col, seg_row, 4, 2, done, after=far_up)
    core_up = plan.gather_core(gate([*near_up, *far_up], done))
    context, logs = attend(projected, seg_col, seg_row, 6, 2, done, after=(line_down,))
    near_down = plan.gather_near(gate(line_down, context))
    w_up = [*near_up, *far_up, *core_up]
    unit, spread, normed_low, *filled = out_up(context, tokens, vectors, up_bias, w_up, places, 2)
    far_down = plan.gather_far(gate(near_down, normed_low))
    core_down = plan.gather_core(gate(near_down, normed_low))
    active, slope = up_rest(normed_low, up_bias, w_up, places, 2, filled, after=near_down[1:])
    w_down = [*near_down, *far_down, *core_down, *plan.gather_core(gate(far_down, active))]
    output, second, grad_branch, grad_up, down_sums, up_terms = down_both(
        unit, cotangent, active, slope, vectors, w_down, places
    )
    core_down = plan.scatter_core([(grad_branch, active[None])])
    first, grad_attn, grad_context, up_sums = up_back(
        unit, spread, second, grad_up, vectors, w_up, places, after=core_down[:1]
    )
    near_down = plan.scatter_near(gate(core_down, grad_attn))
    core_up = plan.scatter_core([(normed_low, grad_up[None])], after=[grad_attn, core_down[-1]])

    def back(first_pair, half_first, earlier, after):
        return attend_back(
            projected, context, grad_context, logs, seg_col, seg_row, first_pair, 2, half_first, 4, earlier, after
        )

    far_down = plan.scatter_far(gate(near_down, core_up[0]))
    grads = back(0, 0, None, near_down[-2:] + core_up[:1])
    near_up = plan.scatter_near(gate(core_up, grads[0]))
    grad_one, sums_one = back(2, 0, grads, core_up[-1:])
    core_one = plan.scatter_core(
        [(context, grad_attn[None]), (tokens, grad_one)], after=far_down[-2:] + near_up[-2:]
    )
    half_down = plan.scatter_half(gate(far_down, core_one[0]))
    far_up = plan.scatter_far(gate(near_up, core_one[0]))
    grads = back(4, 4, None, core_one[:1])
    near_one = plan.scatter_near(core_one)
    grad_two, sums_two = back(6, 4, grads, far_up[-2:] + half_down[-1:] + core_one[-1:])
    half_up = plan.scatter_half(gate(far_up, grad_two))
    line_down = plan.scatter_slab(half_down)
    core_two = plan.scatter_core([(tokens, grad_two)], after=near_one[-2:] + line_down[-1:])
    far_one = plan.scatter_far(gate(near_one, grad_two))
    input_grad = input_back(first, grad_one, grad_two, w_qkv, places, after=core_two[:1])
    head_sums = jnp.concatenate([sums_one, sums_two], axis=0)
    vector_part = jnp.concatenate(
        [
            head_sums[:, 0].reshape(1, D),
            head_sums[:, 1].reshape(1, D),
            up_sums[:3],
            down_sums[:3],
            up_terms.reshape(FF // D, D),
        ],
        axis=0,
    )
    vector_part = plan.total_step(gate(vector_part, core_two[0]), "core")
    near_two = plan.scatter_near(gate(core_two, vector_part, input_grad))
    line_one = plan.scatter_line(gate(far_one, near_two[-2:], half_up[-1]))
    vector_part = plan.total_step(gate(vector_part, near_two[-1]), "x")
    far_two = plan.scatter_far(near_two)
    line_up = plan.scatter_slab(gate(half_up, far_two[-1]))
    line_two = plan.scatter_line(gate(far_two, vector_part))
    vector_part = plan.total_step(gate(vector_part, far_two[-1]), "y")
    down_sum = plan.scatter_end(line_down)
    up_sum = plan.scatter_end(line_up)
    one_sum = plan.scatter_end(line_one)
    vector_part = plan.total_step(vector_part, "near z")
    vector_grad = plan.total_step(vector_part, "far z")
    two_sum = gate(plan.scatter_end(line_two), vector_grad)
    half = D // 2
    out_sum, one_sum = one_sum[:, :D], one_sum[:, D:]
    qkv_sum = [part[:, k * half : (k + 1) * half] for k in range(3) for part in (one_sum, two_sum)]
    summed = jnp.concatenate([*qkv_sum, out_sum, up_sum, down_sum], axis=1)
    stripes = summed.reshape(slab, stripe_count, stripe).transpose(1, 0, 2)
    slot_grad = plan.collect(stripes, stripe_at, heavy)
    keep = lax.dynamic_slice(used, (replica_index * slot_count,), (slot_count,))[:, None, None]
    new_master, new_one, new_two = adamw(
        master, moment_one, moment_two, slot_grad.astype(jnp.float32), rate_matrix, decay_rate
    )
    new_master = jnp.where(keep, new_master, 0.0)
    new_one = jnp.where(keep, new_one, 0.0)
    new_two = jnp.where(keep, new_two, 0.0)
    new_vectors, new_vector_one, new_vector_two = adamw(
        vectors, vector_one, vector_two, vector_grad, rate_vector, 0.0
    )
    return (
        output,
        input_grad,
        new_master,
        new_master.astype(jnp.bfloat16),
        new_one,
        new_two,
        new_vectors,
        new_vector_one,
        new_vector_two,
    )


def solution(mesh):
    return jax.shard_map(
        on_device,
        mesh=mesh,
        in_specs=(
            P(BOTH, None),
            P(BOTH, None),
            P(BOTH, None),
            P(),
            P("replica", "shard", None),
            P("replica", "shard", None),
            P("replica", "shard", None),
            P(),
            P(),
            P(),
        ),
        out_specs=(
            P(BOTH, None),
            P(BOTH, None),
            P("replica", "shard", None),
            P("replica", "shard", None),
            P("replica", "shard", None),
            P("replica", "shard", None),
            P(),
            P(),
            P(),
        ),
        check_vma=False,
    )
```
